32 devices in a mesh: basis: 4 (over x, core), tm: 8 (over z, y).
Axes of the slice: x: 2, y: 2, z: 4, core: 2. Of those that a mesh axis runs over, the one named last changes fastest.
Arguments:
- strain: bfloat16 [3, 4096], P(None, 'tm'), may hold values from -6 to 6
- basis_filters: bfloat16 [4096, 2048], P('basis'), may hold values from -0.125 to 0.125
- coefficients: bfloat16 [8192, 4096], P(('basis', 'tm')), may hold values from -0.1875 to 0.1875
Outputs:
- snr: bfloat16 [8192, 3, 1024], P('basis', None, 'tm')
The draws below stay inside these ranges and needn't reach their ends.
All inputs are finite; a program needn't handle non-finite values.
Results may differ from the reference program's by a relative error of at most 0.0049.
Values may be sent and summed in bfloat16 or wider, within the bound.
No kernel may reach another device: no remote copies, remote signals or barrier semaphores. Data moves between devices by JAX's collectives and lax.ppermute only.
A program may use at most 128 MiB of HBM per device.

```python
import jax
import jax.numpy as jnp
from jax import lax

DET = 3
STRIDE = 4
FLEN = 2048
NBASIS = 4096
TEMPL = 8192
TIMES = 1024
SAMPLES = 4096
N_TM = 8


def with_spikes(entries, key, source, target, parts, factor):
    def block_of(axis_at):
        return (jnp.arange(entries.shape[axis_at]) // (entries.shape[axis_at] // parts)).reshape((-1,) + (1,) * (entries.ndim - 1 - axis_at))

    one_side = jax.random.permutation(key, parts)[block_of(target)]
    second = (block_of(target) + parts // 2) % parts
    return jnp.where((block_of(source) == one_side) | (block_of(source) == second), factor * entries, entries)


def block_scale(own_key, dims, split, low, largest):
    def one(axis_at, shards_of):
        heights = jax.random.uniform(jax.random.fold_in(jax.random.fold_in(own_key, 6), axis_at), (shards_of,), jnp.float32, low / len(split), largest / len(split))
        return jnp.repeat(jnp.exp(heights), dims[axis_at] // shards_of).reshape((-1,) + (1,) * (len(dims) - axis_at - 1))

    factor_of = one(*split[0])
    for cut in split[1:]:
        factor_of = factor_of * one(*cut)
    return factor_of


def scatter_about(key, extent, deviation, bound, pieces=(), dtype=jnp.bfloat16):
    values = deviation * jax.random.normal(key, extent, jnp.float32)
    if pieces:
        values = values * block_scale(key, extent, pieces, -0.22, 0.18)
    return jnp.clip(values, -bound, bound).astype(dtype)


def bell_draw_with(stream_key, extent, spread, limit, split, heavy, held_as=jnp.bfloat16):
    array = spread * jax.random.normal(stream_key, extent, jnp.float32)
    if split:
        array = array * block_scale(stream_key, extent, split, -0.22, 0.18)
    return jnp.clip(with_spikes(array, jax.random.fold_in(stream_key, 3), *heavy), -limit, limit).astype(held_as)


def setup_inputs(seed: int = 0) -> dict:
    seeds = jax.random.split(jax.random.key(seed), 4)
    return {
        "strain": scatter_about(seeds[0], (DET, SAMPLES), 1.0, 6.0, ((1, 8),)),
        "basis_filters": scatter_about(seeds[1], (NBASIS, FLEN), FLEN ** -0.5, 0.125, ((0, 4),)),
        "coefficients": bell_draw_with(seeds[2], (TEMPL, NBASIS), NBASIS ** -0.5, 0.1875, ((0, 32),), (1, 0, 32, 2.75)),
    }


def reference(strain, basis_filters, coefficients):
    total_len = (TIMES + FLEN // STRIDE - 1) * STRIDE
    padded = jnp.pad(strain, ((0, 0), (0, total_len - SAMPLES)))
    window = padded.reshape(DET, total_len // STRIDE, STRIDE)
    phases = basis_filters.reshape(NBASIS, FLEN // STRIDE, STRIDE)
    correlation = lax.conv_general_dilated(window, phases, (1,), "VALID", dimension_numbers=("NHC", "OHI", "NCH"), preferred_element_type=jnp.float32).astype(jnp.bfloat16)
    flat_corr = jnp.transpose(correlation, (1, 0, 2)).reshape(NBASIS, DET * TIMES)
    row_blocks = coefficients.reshape(N_TM, TEMPL // N_TM, NBASIS)

    def one_block(rows_here):
        return jnp.dot(rows_here, flat_corr, preferred_element_type=jnp.float32).astype(jnp.bfloat16)

    result = lax.map(one_block, row_blocks)
    return result.reshape(TEMPL, DET, TIMES)
```

```python
import functools

import jax
import jax.numpy as jnp
from jax import lax
from jax.experimental import pallas as pl
from jax.experimental.pallas import tpu as pltpu
from jax.sharding import PartitionSpec as P

STRIDE = 4
LANES = 128
CHUNKS = 4
VMEM_LIMIT = 48 * 1024 * 1024


def flipped(block, axis, mask):
    return lax.ppermute(block, axis, [(i, i ^ mask) for i in range(lax.axis_size(axis))])


def gathered_phases(strain):
    detectors, here = strain.shape
    steps = here // STRIDE
    phases = strain.reshape(detectors, steps, STRIDE).transpose(0, 2, 1)
    count = lax.axis_size("tm")
    if count & (count - 1):
        return lax.all_gather(phases, "tm", axis=2, tiled=True)
    me = lax.axis_index("tm")
    mask = 1
    while mask < count:
        other = flipped(phases, "tm", mask)
        upper = (me & mask) != 0
        phases = jnp.concatenate(
            [jnp.where(upper, other, phases), jnp.where(upper, phases, other)], axis=2
        )
        mask *= 2
    return phases


def hankel_kernel(rows_ref, out_ref):
    tile = rows_ref[0]
    width = out_ref.shape[2]
    length = tile.shape[1]
    per_step = 16 // STRIDE

    def step(i, carry):
        first = pltpu.roll(tile, lax.rem(length - per_step * i, length), 1)
        second = pltpu.roll(tile, length - per_step * i - per_step // 2, 1)
        block = jnp.concatenate([first[:, :width], second[:, :width]], axis=0)
        out_ref[0, pl.ds(pl.multiple_of(16 * i, 16), 16), :] = block.astype(out_ref.dtype)
        return carry

    lax.fori_loop(0, out_ref.shape[1] // 16, step, 0)


def hankel(phases, taps, depth, times):
    detectors, _, have = phases.shape
    width = times + (taps - depth) // STRIDE
    length = -(-(width + depth // STRIDE) // LANES) * LANES
    padded = jnp.pad(phases.astype(jnp.float32), ((0, 0), (0, 0), (0, length + 1 - have)))
    rows = jnp.concatenate([padded[:, :, :length], padded[:, :, 1:]], axis=1)
    return pl.pallas_call(
        hankel_kernel,
        grid=(detectors,),
        in_specs=[pl.BlockSpec((1, 2 * STRIDE, length), lambda d: (d, 0, 0))],
        out_specs=pl.BlockSpec((1, depth, width), lambda d: (d, 0, 0)),
        out_shape=jax.ShapeDtypeStruct((detectors, depth, width), jnp.bfloat16),
        compiler_params=pltpu.CompilerParams(vmem_limit_bytes=VMEM_LIMIT),
        name="hankel",
    )(rows)


def partial_kernel(rows_ref, near_ref, far_ref, out_ref):
    half = near_ref.shape[0]
    total = jnp.dot(rows_ref[:, :half], near_ref[...], preferred_element_type=jnp.float32)
    total += jnp.dot(rows_ref[:, half:], far_ref[...], preferred_element_type=jnp.float32)
    out_ref[...] = total.astype(out_ref.dtype)


def partial_rows(rows, near, far, dtype):
    count, depth = rows.shape
    half, taps = near.shape
    block = 512
    return pl.pallas_call(
        partial_kernel,
        grid=(taps // block,),
        in_specs=[
            pl.BlockSpec((count, depth), lambda n: (0, 0)),
            pl.BlockSpec((half, block), lambda n: (0, n)),
            pl.BlockSpec((half, block), lambda n: (0, n)),
        ],
        out_specs=pl.BlockSpec((count, block), lambda n: (0, n)),
        out_shape=jax.ShapeDtypeStruct((count, taps), dtype),
        cost_estimate=pl.CostEstimate(
            flops=2 * count * depth * taps, bytes_accessed=2 * depth * taps, transcendentals=0
        ),
        compiler_params=pltpu.CompilerParams(vmem_limit_bytes=VMEM_LIMIT),
        name="partial_rows",
    )(rows, near, far)


def product(weights, hankel_ref, start, size):
    depth = hankel_ref.shape[1]
    total = None
    for q in range(weights.shape[1] // depth):
        columns = pl.ds(pl.multiple_of(start + q * (depth // STRIDE), LANES), size)
        term = jnp.dot(
            weights[:, q * depth : (q + 1) * depth],
            hankel_ref[0, :, columns],
            preferred_element_type=jnp.float32,
        )
        total = term if total is None else total + term
    return total


def series_kernel(me_ref, own_ref, other_ref, hankel_ref, *outs):
    weights = (own_ref[...] + other_ref[...].astype(jnp.float32)).astype(jnp.bfloat16)
    me = me_ref[0]
    low = lax.rem(me, 2)
    here = outs[0].shape[2]
    for k in range(0, len(outs), 2):
        pair = (me ^ k) // 2
        total = product(weights, hankel_ref, pair * (2 * here), 2 * here).astype(jnp.bfloat16)
        left, right = total[:, :here], total[:, here:]
        outs[k][0] = jnp.where(low == 0, left, right)
        outs[k + 1][0] = jnp.where(low == 0, right, left)


def series(me, own, other, which, hankel_matrix, count, here):
    rows, taps = other.shape
    detectors, depth, width = hankel_matrix.shape
    return pl.pallas_call(
        series_kernel,
        grid_spec=pltpu.PrefetchScalarGridSpec(
            num_scalar_prefetch=1,
            grid=(detectors,),
            in_specs=[
                pl.BlockSpec((rows, taps), lambda d, me: (which, 0)),
                pl.BlockSpec((rows, taps), lambda d, me: (0, 0)),
                pl.BlockSpec((1, depth, width), lambda d, me: (d, 0, 0)),
            ],
            out_specs=[pl.BlockSpec((1, rows, here), lambda d, me: (d, 0, 0))] * count,
        ),
        out_shape=[jax.ShapeDtypeStruct((detectors, rows, here), jnp.bfloat16)] * count,
        cost_estimate=pl.CostEstimate(
            flops=2 * rows * taps * detectors * count * here,
            bytes_accessed=2 * detectors * depth * width,
            transcendentals=0,
        ),
        compiler_params=pltpu.CompilerParams(vmem_limit_bytes=VMEM_LIMIT),
        name="series",
    )(me, own, other, hankel_matrix)


def long_series_kernel(own_ref, other_ref, hankel_ref, out_ref):
    weights = (own_ref[...] + other_ref[...].astype(jnp.float32)).astype(jnp.bfloat16)
    here = out_ref.shape[3]
    total = product(weights, hankel_ref, pl.program_id(1) * (2 * here), 2 * here)
    out_ref[0, 0] = total[:, :here].astype(jnp.bfloat16)
    out_ref[1, 0] = total[:, here:].astype(jnp.bfloat16)


def long_series(own, other, which, hankel_matrix, count, here):
    rows, taps = other.shape
    detectors, depth, width = hankel_matrix.shape
    return pl.pallas_call(
        long_series_kernel,
        grid=(detectors, count // 2),
        in_specs=[
            pl.BlockSpec((rows, taps), lambda d, n: (which, 0)),
            pl.BlockSpec((rows, taps), lambda d, n: (0, 0)),
            pl.BlockSpec((1, depth, width), lambda d, n: (d, 0, 0)),
        ],
        out_specs=pl.BlockSpec((2, 1, rows, here), lambda d, n: (n, d, 0, 0)),
        out_shape=jax.ShapeDtypeStruct((count, detectors, rows, here), jnp.bfloat16),
        compiler_params=pltpu.CompilerParams(vmem_limit_bytes=VMEM_LIMIT),
        name="long_series",
    )(own, other, hankel_matrix)


def shards(strain, basis_filters, coefficients):
    detectors, samples_here = strain.shape
    here = samples_here // STRIDE
    filters, taps = basis_filters.shape
    own_rows = coefficients.shape[0]
    count = lax.axis_size("tm")
    me = lax.axis_index("tm")
    group = lax.axis_index("basis")
    chunks = min(CHUNKS, own_rows // 16)
    rows = own_rows // chunks

    def columns(first, size, which):
        return lax.dynamic_slice(coefficients, (first, which * filters), (size, filters))

    def both(first, size, which):
        return jnp.concatenate([columns(first, size, which), columns(first, size, which ^ 1)], axis=1)

    asked = [flipped(both(c * rows, rows, group ^ 2), "basis", 2) for c in range(chunks)]
    sibling = flipped(basis_filters, "basis", 1)
    matrix = hankel(gathered_phases(strain), taps, 4 * LANES, count * here)
    own = partial_rows(both(0, own_rows, group), basis_filters, sibling, jnp.float32)

    result = jnp.zeros((detectors, count * own_rows, here), jnp.bfloat16)
    for c in range(chunks):
        answer = partial_rows(asked[c], basis_filters, sibling, jnp.bfloat16)
        other = flipped(answer, "basis", 2)
        if count == 8:
            blocks = series(jnp.full((1,), me, jnp.int32), own, other, c, matrix, count, here)
            for k, block in enumerate(blocks):
                arrived = flipped(block, "tm", k) if k else block
                result = lax.dynamic_update_slice(result, arrived, (0, (me ^ k) * own_rows + c * rows, 0))
        else:
            blocks = long_series(own, other, c, matrix, count, here)
            arrived = lax.all_to_all(blocks, "tm", split_axis=0, concat_axis=0, tiled=True)
            for k in range(count):
                result = lax.dynamic_update_slice(result, arrived[k], (0, k * own_rows + c * rows, 0))
    return result.transpose(1, 0, 2)


def solution(mesh):
    placed = (P(None, "tm"), P("basis", None), P(("basis", "tm"), None))
    return jax.shard_map(
        shards, mesh=mesh, in_specs=placed, out_specs=P("basis", None, "tm"), check_vma=False
    )
```

```python
import functools

import jax
import jax.numpy as jnp
from jax import lax
from jax.experimental import pallas as pl
from jax.experimental.pallas import tpu as pltpu
from jax.sharding import PartitionSpec as P

STRIDE = 4
LANES = 128
DEPTH = 4 * LANES
MIB = 1024 * 1024
GROUPS = [[128], [128]]


def flipped(block, axis, mask):
    return lax.ppermute(block, axis, [(i, i ^ mask) for i in range(lax.axis_size(axis))])


def after(value, *others):
    return lax.optimization_barrier((value, *others))[0]


def in_vmem(array):
    return pltpu.with_memory_space_constraint(array, pltpu.VMEM)


def in_hbm(array):
    return pltpu.with_memory_space_constraint(array, pltpu.HBM)


def whole_in_vmem(count):
    return [pl.BlockSpec(memory_space=pltpu.VMEM)] * count


def strain_doublings(strain):
    steps = [strain[None]]
    mask = 1
    while mask < lax.axis_size("tm"):
        steps.append(jnp.concatenate([steps[-1], flipped(steps[-1], "tm", mask)], axis=0))
        mask *= 2
    return steps


def shifted(tile, distance):
    return pltpu.roll(tile, tile.shape[1] - distance, 1) if distance else tile


def hankel_kernel(strain_ref, out_ref, split_ref, tile_ref):
    count, detectors, samples = strain_ref.shape
    here = samples // STRIDE
    width = out_ref.shape[2]
    me = lax.axis_index("tm")
    sample = lax.broadcasted_iota(jnp.int32, (samples, samples), 0)
    column = lax.broadcasted_iota(jnp.int32, (samples, samples), 1)
    wanted = STRIDE * lax.rem(column, here) + column // here
    selector = jnp.where(sample == wanted, 1.0, 0.0).astype(jnp.bfloat16)
    for k in range(count):
        split_ref[k] = jnp.dot(strain_ref[k], selector, preferred_element_type=jnp.float32)
    tile_ref[...] = jnp.zeros_like(tile_ref)
    for t in range(count):
        block = split_ref[me ^ t]
        for d in range(detectors):
            for p in range(STRIDE):
                tile_ref[d, p : p + 1, t * here : (t + 1) * here] = block[
                    d : d + 1, p * here : (p + 1) * here
                ]
    per_half = 8 // STRIDE
    row = lax.broadcasted_iota(jnp.int32, tile_ref.shape[1:], 0)
    for d in range(detectors):
        tile = tile_ref[d]
        tile = jnp.where(row < STRIDE, tile, pltpu.roll(shifted(tile, 1), STRIDE, 0))
        for i in range(out_ref.shape[1] // 16):
            first = shifted(tile, 2 * per_half * i)
            second = shifted(tile, 2 * per_half * i + per_half)
            block = jnp.concatenate([first[:, :width], second[:, :width]], axis=0)
            out_ref[d, 16 * i : 16 * (i + 1), :] = block.astype(out_ref.dtype)


def hankel(blocks, taps):
    count, detectors, samples = blocks.shape
    width = count * samples // STRIDE + (taps - DEPTH) // STRIDE
    length = -(-(width + DEPTH // STRIDE) // LANES) * LANES
    return pl.pallas_call(
        hankel_kernel,
        in_specs=whole_in_vmem(1),
        out_specs=pl.BlockSpec(memory_space=pltpu.VMEM),
        out_shape=jax.ShapeDtypeStruct((detectors, DEPTH, width), jnp.bfloat16),
        scratch_shapes=[
            pltpu.VMEM((count, detectors, samples), jnp.float32),
            pltpu.VMEM((detectors, 2 * STRIDE, length), jnp.float32),
        ],
        compiler_params=pltpu.CompilerParams(vmem_limit_bytes=16 * MIB),
        name="hankel",
    )(in_vmem(blocks))


def long_hankel_kernel(rows_ref, out_ref):
    tile = rows_ref[0]
    width = out_ref.shape[2]
    length = tile.shape[1]
    per_half = 8 // STRIDE

    def step(i, carry):
        first = pltpu.roll(tile, lax.rem(length - 2 * per_half * i, length), 1)
        second = pltpu.roll(tile, length - 2 * per_half * i - per_half, 1)
        block = jnp.concatenate([first[:, :width], second[:, :width]], axis=0)
        out_ref[0, pl.ds(pl.multiple_of(16 * i, 16), 16), :] = block.astype(out_ref.dtype)
        return carry

    lax.fori_loop(0, out_ref.shape[1] // 16, step, 0)


def long_hankel(strain, taps, times):
    detectors, here = strain.shape
    phases = strain.reshape(detectors, here // STRIDE, STRIDE).transpose(0, 2, 1)
    phases = lax.all_gather(phases, "tm", axis=2, tiled=True)
    width = times + (taps - DEPTH) // STRIDE
    length = -(-(width + DEPTH // STRIDE) // LANES) * LANES
    padded = jnp.pad(phases.astype(jnp.float32), ((0, 0), (0, 0), (0, length + 1 - times)))
    rows = jnp.concatenate([padded[:, :, :length], padded[:, :, 1:]], axis=1)
    return pl.pallas_call(
        long_hankel_kernel,
        grid=(detectors,),
        in_specs=[pl.BlockSpec((1, 2 * STRIDE, length), lambda d: (d, 0, 0))],
        out_specs=pl.BlockSpec((1, DEPTH, width), lambda d: (d, 0, 0)),
        out_shape=jax.ShapeDtypeStruct((detectors, DEPTH, width), jnp.bfloat16),
        compiler_params=pltpu.CompilerParams(vmem_limit_bytes=24 * MIB),
        name="long_hankel",
    )(rows)


def staging_kernel(coefficients_ref, near_ref, far_ref, filters_ref, own_ref, rows_ref, semaphores):
    half, taps = near_ref.shape
    block = taps // 4
    group = lax.axis_index("basis")
    copies = []
    for i, which in enumerate((group, group ^ 1)):
        columns = pl.ds(pl.multiple_of(which * half, LANES), half)
        copies.append(
            pltpu.make_async_copy(
                coefficients_ref.at[:, columns],
                rows_ref.at[:, i * half : (i + 1) * half],
                semaphores.at[i],
            )
        )
    for n in range(4):
        for i, source in enumerate((near_ref, far_ref)):
            there = filters_ref.at[i * half : (i + 1) * half, n * block : (n + 1) * block]
            copies.append(
                pltpu.make_async_copy(
                    source.at[:, n * block : (n + 1) * block], there, semaphores.at[2 + 2 * n + i]
                )
            )
    for copy in copies:
        copy.start()
    copies[0].wait()
    copies[1].wait()
    for n in range(4):
        copies[2 + 2 * n].wait()
        copies[3 + 2 * n].wait()
        own_ref[:, n * block : (n + 1) * block] = jnp.dot(
            rows_ref[...],
            filters_ref[:, n * block : (n + 1) * block],
            preferred_element_type=jnp.float32,
        )


def staged(coefficients, near, far):
    own_rows = coefficients.shape[0]
    half, taps = near.shape
    return pl.pallas_call(
        staging_kernel,
        in_specs=[pl.BlockSpec(memory_space=pl.ANY)] * 3,
        out_specs=whole_in_vmem(2),
        out_shape=[
            jax.ShapeDtypeStruct((2 * half, taps), jnp.bfloat16),
            jax.ShapeDtypeStruct((own_rows, taps), jnp.float32),
        ],
        scratch_shapes=[
            pltpu.VMEM((own_rows, 2 * half), jnp.bfloat16),
            pltpu.SemaphoreType.DMA((10,)),
        ],
        cost_estimate=pl.CostEstimate(
            flops=4 * own_rows * half * taps, bytes_accessed=8 * half * taps, transcendentals=0
        ),
        compiler_params=pltpu.CompilerParams(vmem_limit_bytes=20 * MIB),
        name="staged",
    )(in_hbm(coefficients), in_hbm(near), in_hbm(far))


def partial_kernel(rows_ref, filters_ref, out_ref):
    depth, taps = filters_ref.shape
    core = lax.rem(lax.axis_index("basis"), 2)
    near = pl.ds(pl.multiple_of(core * (depth // 2), LANES), depth // 2)
    far = pl.ds(pl.multiple_of((1 - core) * (depth // 2), LANES), depth // 2)
    rows = jnp.concatenate([rows_ref[:, near], rows_ref[:, far]], axis=1)
    for n in range(0, taps, 512):
        out_ref[:, n : n + 512] = jnp.dot(
            rows, filters_ref[:, n : n + 512], preferred_element_type=jnp.float32
        ).astype(out_ref.dtype)


def partial_rows(rows, filters):
    count = rows.shape[0]
    depth, taps = filters.shape
    return pl.pallas_call(
        partial_kernel,
        in_specs=whole_in_vmem(2),
        out_specs=pl.BlockSpec(memory_space=pltpu.VMEM),
        out_shape=jax.ShapeDtypeStruct((count, taps), jnp.bfloat16),
        cost_estimate=pl.CostEstimate(
            flops=2 * count * depth * taps, bytes_accessed=2 * depth * taps, transcendentals=0
        ),
        compiler_params=pltpu.CompilerParams(vmem_limit_bytes=16 * MIB),
        name="partial_rows",
    )(in_vmem(rows), in_vmem(filters))


def rounded_sum(own, others):
    other = jnp.concatenate([ref[...] for ref in others], axis=0)
    return (own + other.astype(jnp.float32)).astype(jnp.bfloat16)


def series_kernel(start, parts, own_ref, *refs):
    others, hankel_ref, outs, scratch = refs[:parts], refs[parts], refs[parts + 1 : -1], refs[-1]
    detectors = hankel_ref.shape[0]
    rows, times = scratch.shape
    taps = own_ref.shape[1]
    here = times // len(outs)
    me = lax.axis_index("tm")
    weights = rounded_sum(own_ref[start : start + rows], others)
    for d in range(detectors):
        total = None
        for q in range(taps // DEPTH):
            term = jnp.dot(
                weights[:, q * DEPTH : (q + 1) * DEPTH],
                hankel_ref[d, :, q * LANES : q * LANES + times],
                preferred_element_type=jnp.float32,
            )
            total = term if total is None else total + term
        scratch[...] = total.astype(jnp.bfloat16)
        for k, out in enumerate(outs):
            out[d] = scratch[:, pl.ds(pl.multiple_of((me ^ k) * here, LANES), here)]


def series(own, start, others, matrix, count, here):
    taps = own.shape[1]
    rows = sum(part.shape[0] for part in others)
    detectors, depth, width = matrix.shape
    return pl.pallas_call(
        functools.partial(series_kernel, start, len(others)),
        in_specs=whole_in_vmem(2 + len(others)),
        out_specs=whole_in_vmem(count),
        out_shape=[jax.ShapeDtypeStruct((detectors, rows, here), jnp.bfloat16)] * count,
        scratch_shapes=[pltpu.VMEM((rows, count * here), jnp.bfloat16)],
        cost_estimate=pl.CostEstimate(
            flops=2 * rows * taps * detectors * count * here,
            bytes_accessed=2 * detectors * depth * width,
            transcendentals=0,
        ),
        compiler_params=pltpu.CompilerParams(vmem_limit_bytes=16 * MIB),
        name="series",
    )(in_vmem(own), *[in_vmem(part) for part in others], in_vmem(matrix))


def assembling_kernel(starts, own_rows, *refs):
    blocks, out_ref, semaphores = refs[:-2], refs[-2], refs[-1]
    count = len(blocks) // len(starts)
    me = lax.axis_index("tm")
    copies = []
    for g, start in enumerate(starts):
        for k in range(count):
            block = blocks[g * count + k]
            at = pl.multiple_of((me ^ k) * own_rows + start, 16)
            copies.append(
                pltpu.make_async_copy(
                    block,
                    out_ref.at[:, pl.ds(at, block.shape[1]), :],
                    semaphores.at[g * count + k],
                )
            )
    for copy in copies:
        copy.start()
    for copy in copies:
        copy.wait()


def assembled(groups, own_rows):
    count = len(groups[0])
    detectors, _, here = groups[0][0].shape
    starts, start = [], 0
    for group in groups:
        starts.append(start)
        start += group[0].shape[1]
    blocks = [block for group in groups for block in group]
    return pl.pallas_call(
        functools.partial(assembling_kernel, starts, own_rows),
        in_specs=whole_in_vmem(len(blocks)),
        out_specs=pl.BlockSpec(memory_space=pl.ANY),
        out_shape=jax.ShapeDtypeStruct((detectors, count * own_rows, here), jnp.bfloat16),
        scratch_shapes=[pltpu.SemaphoreType.DMA((len(blocks),))],
        compiler_params=pltpu.CompilerParams(vmem_limit_bytes=16 * MIB),
        name="assembled",
    )(*[in_vmem(block) for block in blocks])


def long_series_kernel(weights_ref, hankel_ref, out_ref):
    here = out_ref.shape[3]
    start = pl.program_id(1) * (2 * here)
    total = None
    for q in range(weights_ref.shape[1] // DEPTH):
        columns = pl.ds(pl.multiple_of(start + q * LANES, LANES), 2 * here)
        term = jnp.dot(
            weights_ref[:, q * DEPTH : (q + 1) * DEPTH],
            hankel_ref[0, :, columns],
            preferred_element_type=jnp.float32,
        )
        total = term if total is None else total + term
    out_ref[0, 0] = total[:, :here].astype(jnp.bfloat16)
    out_ref[1, 0] = total[:, here:].astype(jnp.bfloat16)


def long_series(weights, matrix, count, here):
    rows, taps = weights.shape
    detectors, depth, width = matrix.shape
    return pl.pallas_call(
        long_series_kernel,
        grid=(detectors, count // 2),
        in_specs=[
            pl.BlockSpec((rows, taps), lambda d, n: (0, 0)),
            pl.BlockSpec((1, depth, width), lambda d, n: (d, 0, 0)),
        ],
        out_specs=pl.BlockSpec((2, 1, rows, here), lambda d, n: (n, d, 0, 0)),
        out_shape=jax.ShapeDtypeStruct((count, detectors, rows, here), jnp.bfloat16),
        compiler_params=pltpu.CompilerParams(vmem_limit_bytes=32 * MIB),
        name="long_series",
    )(weights, matrix)


def shards(strain, basis_filters, coefficients):
    detectors, samples_here = strain.shape
    here = samples_here // STRIDE
    filters, taps = basis_filters.shape
    own_rows = coefficients.shape[0]
    count = lax.axis_size("tm")
    me = lax.axis_index("tm")
    group = lax.axis_index("basis")
    short = count == 8 and here == LANES
    groups = GROUPS if short and own_rows == 256 else [[own_rows]]
    sizes = [size for part in groups for size in part]
    starts = [sum(sizes[:c]) for c in range(len(sizes))]
    chunks = range(len(sizes))

    at = (group // 2 ^ 1) * (2 * filters)
    cuts = []
    for c in chunks:
        source = after(coefficients, cuts[-1]) if cuts else coefficients
        cuts.append(lax.dynamic_slice(source, (starts[c], at), (sizes[c], 2 * filters)))
    asked = [flipped(cut, "basis", 2) for cut in cuts]
    sibling = flipped(basis_filters, "basis", 1)
    if short:
        steps = strain_doublings(after(strain, cuts[-1]))
        chip_filters, own = staged(after(coefficients, steps[1]), basis_filters, sibling)
        matrix = hankel(steps[-1], taps)
        asked[0] = after(asked[0], steps[2])
        asked[-1] = after(asked[-1], matrix)
    else:
        chip_filters, own = staged(coefficients, basis_filters, sibling)
        matrix = long_hankel(strain, taps, count * here)
    other = [flipped(partial_rows(rows, chip_filters), "basis", 2) for rows in asked]

    if not short:
        weights = (own + other[0].astype(jnp.float32)).astype(jnp.bfloat16)
        blocks = long_series(weights, matrix, count, here)
        arrived = lax.all_to_all(blocks, "tm", split_axis=0, concat_axis=0, tiled=True)
        return arrived.transpose(0, 2, 1, 3).reshape(count * own_rows, detectors, here)

    blocks = []
    c = 0
    for part in groups:
        blocks.append(series(own, starts[c], other[c : c + len(part)], matrix, count, here))
        c += len(part)
    arrived = [[flipped(b[k], "tm", k) if k else b[k] for k in range(count)] for b in blocks]
    return assembled(arrived, own_rows).transpose(1, 0, 2)


def solution(mesh):
    placed = (P(None, "tm"), P("basis", None), P(("basis", "tm"), None))
    return jax.shard_map(
        shards, mesh=mesh, in_specs=placed, out_specs=P("basis", None, "tm"), check_vma=False
    )
```

```python
import functools

import jax
import jax.numpy as jnp
from jax import lax
from jax.experimental import pallas as pl
from jax.experimental.pallas import tpu as pltpu
from jax.sharding import PartitionSpec as P

STRIDE = 4
LANES = 128
DEPTH = 4 * LANES
MIB = 1024 * 1024
COST = pl.CostEstimate(flops=1, bytes_accessed=1, transcendentals=0)
SIZES = [64, 64, 64, 64]


def flipped(block, axis, mask):
    return lax.ppermute(block, axis, [(i, i ^ mask) for i in range(lax.axis_size(axis))])


def after(value, *others):
    return lax.optimization_barrier((value, *others))[0]


def in_vmem(array):
    return pltpu.with_memory_space_constraint(array, pltpu.VMEM)


def in_hbm(array):
    return pltpu.with_memory_space_constraint(array, pltpu.HBM)


def whole_in_vmem(count):
    return [pl.BlockSpec(memory_space=pltpu.VMEM)] * count


def doubled(blocks):
    return jnp.concatenate([blocks, flipped(blocks, "tm", blocks.shape[0])], axis=0)


def shifted(tile, distance):
    return pltpu.roll(tile, tile.shape[1] - distance, 1) if distance else tile


def hankel_kernel(strain_ref, out_ref, split_ref, tile_ref):
    count, detectors, samples = strain_ref.shape
    here = samples // STRIDE
    width = out_ref.shape[2]
    me = lax.axis_index("tm")
    sample = lax.broadcasted_iota(jnp.int32, (samples, samples), 0)
    column = lax.broadcasted_iota(jnp.int32, (samples, samples), 1)
    wanted = STRIDE * lax.rem(column, here) + column // here
    selector = jnp.where(sample == wanted, 1.0, 0.0).astype(jnp.bfloat16)
    for k in range(count):
        split_ref[k] = jnp.dot(strain_ref[k], selector, preferred_element_type=jnp.float32)
    tile_ref[...] = jnp.zeros_like(tile_ref)
    for t in range(count):
        block = split_ref[me ^ t]
        for d in range(detectors):
            for p in range(STRIDE):
                tile_ref[d, p : p + 1, t * here : (t + 1) * here] = block[
                    d : d + 1, p * here : (p + 1) * here
                ]
    per_half = 8 // STRIDE
    row = lax.broadcasted_iota(jnp.int32, tile_ref.shape[1:], 0)
    for d in range(detectors):
        tile = tile_ref[d]
        tile = jnp.where(row < STRIDE, tile, pltpu.roll(shifted(tile, 1), STRIDE, 0))
        for i in range(out_ref.shape[1] // 16):
            first = shifted(tile, 2 * per_half * i)
            second = shifted(tile, 2 * per_half * i + per_half)
            block = jnp.concatenate([first[:, :width], second[:, :width]], axis=0)
            out_ref[d, 16 * i : 16 * (i + 1), :] = block.astype(out_ref.dtype)


def hankel(blocks, taps):
    count, detectors, samples = blocks.shape
    width = count * samples // STRIDE + (taps - DEPTH) // STRIDE
    length = -(-(width + DEPTH // STRIDE) // LANES) * LANES
    return pl.pallas_call(
        hankel_kernel,
        in_specs=whole_in_vmem(1),
        out_specs=pl.BlockSpec(memory_space=pltpu.VMEM),
        out_shape=jax.ShapeDtypeStruct((detectors, DEPTH, width), jnp.bfloat16),
        scratch_shapes=[
            pltpu.VMEM((count, detectors, samples), jnp.float32),
            pltpu.VMEM((detectors, 2 * STRIDE, length), jnp.float32),
        ],
        cost_estimate=COST,
        compiler_params=pltpu.CompilerParams(vmem_limit_bytes=16 * MIB),
        name="hankel",
    )(in_vmem(blocks))


def long_hankel_kernel(rows_ref, out_ref):
    tile = rows_ref[0]
    width = out_ref.shape[2]
    length = tile.shape[1]
    per_half = 8 // STRIDE

    def step(i, carry):
        first = pltpu.roll(tile, lax.rem(length - 2 * per_half * i, length), 1)
        second = pltpu.roll(tile, length - 2 * per_half * i - per_half, 1)
        block = jnp.concatenate([first[:, :width], second[:, :width]], axis=0)
        out_ref[0, pl.ds(pl.multiple_of(16 * i, 16), 16), :] = block.astype(out_ref.dtype)
        return carry

    lax.fori_loop(0, out_ref.shape[1] // 16, step, 0)


def long_hankel(strain, taps, times):
    detectors, here = strain.shape
    phases = strain.reshape(detectors, here // STRIDE, STRIDE).transpose(0, 2, 1)
    phases = lax.all_gather(phases, "tm", axis=2, tiled=True)
    width = times + (taps - DEPTH) // STRIDE
    length = -(-(width + DEPTH // STRIDE) // LANES) * LANES
    padded = jnp.pad(phases.astype(jnp.float32), ((0, 0), (0, 0), (0, length + 1 - times)))
    rows = jnp.concatenate([padded[:, :, :length], padded[:, :, 1:]], axis=1)
    return pl.pallas_call(
        long_hankel_kernel,
        grid=(detectors,),
        in_specs=[pl.BlockSpec((1, 2 * STRIDE, length), lambda d: (d, 0, 0))],
        out_specs=pl.BlockSpec((1, DEPTH, width), lambda d: (d, 0, 0)),
        out_shape=jax.ShapeDtypeStruct((detectors, DEPTH, width), jnp.bfloat16),
        cost_estimate=COST,
        compiler_params=pltpu.CompilerParams(vmem_limit_bytes=24 * MIB),
        name="long_hankel",
    )(rows)


def staging_kernel(coefficients_ref, near_ref, far_ref, filters_ref, own_ref, rows_ref, semaphores):
    half, taps = near_ref.shape
    block = taps // 4
    group = lax.axis_index("basis")
    copies = []
    for i, which in enumerate((group, group ^ 1)):
        columns = pl.ds(pl.multiple_of(which * half, LANES), half)
        copies.append(
            pltpu.make_async_copy(
                coefficients_ref.at[:, columns],
                rows_ref.at[:, i * half : (i + 1) * half],
                semaphores.at[i],
            )
        )
    for n in range(4):
        for i, source in enumerate((near_ref, far_ref)):
            there = filters_ref.at[i * half : (i + 1) * half, n * block : (n + 1) * block]
            copies.append(
                pltpu.make_async_copy(
                    source.at[:, n * block : (n + 1) * block], there, semaphores.at[2 + 2 * n + i]
                )
            )
    for copy in copies:
        copy.start()
    copies[0].wait()
    copies[1].wait()
    for n in range(4):
        copies[2 + 2 * n].wait()
        copies[3 + 2 * n].wait()
        own_ref[:, n * block : (n + 1) * block] = jnp.dot(
            rows_ref[...],
            filters_ref[:, n * block : (n + 1) * block],
            preferred_element_type=jnp.float32,
        )


def staged(coefficients, near, far):
    own_rows = coefficients.shape[0]
    half, taps = near.shape
    return pl.pallas_call(
        staging_kernel,
        in_specs=[pl.BlockSpec(memory_space=pl.ANY)] * 3,
        out_specs=whole_in_vmem(2),
        out_shape=[
            jax.ShapeDtypeStruct((2 * half, taps), jnp.bfloat16),
            jax.ShapeDtypeStruct((own_rows, taps), jnp.float32),
        ],
        scratch_shapes=[
            pltpu.VMEM((own_rows, 2 * half), jnp.bfloat16),
            pltpu.SemaphoreType.DMA((10,)),
        ],
        cost_estimate=COST,
        compiler_params=pltpu.CompilerParams(vmem_limit_bytes=20 * MIB),
        name="staged",
    )(in_hbm(coefficients), in_hbm(near), in_hbm(far))


def partial_kernel(rows_ref, filters_ref, out_ref):
    depth, taps = filters_ref.shape
    core = lax.rem(lax.axis_index("basis"), 2)
    near = pl.ds(pl.multiple_of(core * (depth // 2), LANES), depth // 2)
    far = pl.ds(pl.multiple_of((1 - core) * (depth // 2), LANES), depth // 2)
    rows = jnp.concatenate([rows_ref[:, near], rows_ref[:, far]], axis=1)
    for n in range(0, taps, 512):
        out_ref[:, n : n + 512] = jnp.dot(
            rows, filters_ref[:, n : n + 512], preferred_element_type=jnp.float32
        ).astype(out_ref.dtype)


def partial_rows(rows, filters):
    count = rows.shape[0]
    depth, taps = filters.shape
    return pl.pallas_call(
        partial_kernel,
        in_specs=whole_in_vmem(2),
        out_specs=pl.BlockSpec(memory_space=pltpu.VMEM),
        out_shape=jax.ShapeDtypeStruct((count, taps), jnp.bfloat16),
        cost_estimate=COST,
        compiler_params=pltpu.CompilerParams(vmem_limit_bytes=16 * MIB),
        name="partial_rows",
    )(in_vmem(rows), in_vmem(filters))


def series_kernel(start, parts, far, targets, own_ref, *refs):
    others, hankel_ref, outs, scratch = refs[:parts], refs[parts], refs[parts + 1 : -1], refs[-1]
    detectors = hankel_ref.shape[0]
    rows, times = scratch.shape
    taps = own_ref.shape[1]
    here = outs[0].shape[-1]
    near = times // here
    me = lax.axis_index("tm")
    half = me // near
    first = (1 - half if far else half) * times
    other = jnp.concatenate([ref[...] for ref in others], axis=0)
    weights = (own_ref[start : start + rows] + other.astype(jnp.float32)).astype(jnp.bfloat16)
    for d in range(detectors):
        total = None
        for q in range(taps // DEPTH):
            columns = pl.ds(pl.multiple_of(first + q * LANES, LANES), times)
            term = jnp.dot(
                weights[:, q * DEPTH : (q + 1) * DEPTH],
                hankel_ref[d, :, columns],
                preferred_element_type=jnp.float32,
            )
            total = term if total is None else total + term
        scratch[...] = total.astype(jnp.bfloat16)
        for out, target in zip(outs, targets):
            for s, k in enumerate(target):
                at = pl.multiple_of(lax.rem(me ^ k, near) * here, LANES)
                out[s, d] = scratch[:, pl.ds(at, here)]


def series(own, start, others, matrix, here, targets):
    taps = own.shape[1]
    rows = sum(part.shape[0] for part in others)
    detectors = matrix.shape[0]
    near = 4
    far = targets[0][0] >= near
    shapes = [(len(target), detectors, rows, here) for target in targets]
    return pl.pallas_call(
        functools.partial(series_kernel, start, len(others), far, targets),
        in_specs=whole_in_vmem(2 + len(others)),
        out_specs=whole_in_vmem(len(targets)),
        out_shape=[jax.ShapeDtypeStruct(shape, jnp.bfloat16) for shape in shapes],
        scratch_shapes=[pltpu.VMEM((rows, near * here), jnp.bfloat16)],
        cost_estimate=COST,
        compiler_params=pltpu.CompilerParams(vmem_limit_bytes=16 * MIB),
        name="series",
    )(in_vmem(own), *[in_vmem(part) for part in others], in_vmem(matrix))


def second_halves_kernel(counts, *refs):
    ins, out_ref = list(refs[:-1]), refs[-1]
    for k, count in enumerate(counts):
        start = 0
        for ref in ins[:count]:
            rows = ref.shape[2]
            out_ref[k, :, start : start + rows] = ref[1]
            start += rows
        ins = ins[count:]


def second_halves(columns):
    detectors, _, here = columns[0][0].shape[1:]
    rows = sum(pair.shape[2] for pair in columns[0])
    pairs = [pair for column in columns for pair in column]
    return pl.pallas_call(
        functools.partial(second_halves_kernel, [len(column) for column in columns]),
        in_specs=whole_in_vmem(len(pairs)),
        out_specs=pl.BlockSpec(memory_space=pltpu.VMEM),
        out_shape=jax.ShapeDtypeStruct((len(columns), detectors, rows, here), jnp.bfloat16),
        cost_estimate=COST,
        compiler_params=pltpu.CompilerParams(vmem_limit_bytes=16 * MIB),
        name="second_halves",
    )(*[in_vmem(pair) for pair in pairs])


def assembling_kernel(places, own_rows, *refs):
    blocks, out_ref, semaphores = refs[:-2], refs[-2], refs[-1]
    me = lax.axis_index("tm")
    copies = []
    for i, (operand, index, k, start) in enumerate(places):
        block = blocks[operand].at[index]
        rows = block.shape[1]
        at = pl.multiple_of((me ^ k) * own_rows + start, 16)
        copies.append(
            pltpu.make_async_copy(
                block, out_ref.at[:, pl.ds(at, rows), :], semaphores.at[i]
            )
        )
    for copy in copies:
        copy.start()
    for copy in copies:
        copy.wait()


def assembled(operands, places, count, own_rows):
    detectors, _, here = operands[0].shape[-3:]
    return pl.pallas_call(
        functools.partial(assembling_kernel, places, own_rows),
        in_specs=whole_in_vmem(len(operands)),
        out_specs=pl.BlockSpec(memory_space=pl.ANY),
        out_shape=jax.ShapeDtypeStruct((detectors, count * own_rows, here), jnp.bfloat16),
        scratch_shapes=[pltpu.SemaphoreType.DMA((len(places),))],
        cost_estimate=COST,
        compiler_params=pltpu.CompilerParams(vmem_limit_bytes=16 * MIB),
        name="assembled",
    )(*[in_vmem(operand) for operand in operands])


def long_series_kernel(weights_ref, hankel_ref, out_ref):
    here = out_ref.shape[3]
    start = pl.program_id(1) * (2 * here)
    total = None
    for q in range(weights_ref.shape[1] // DEPTH):
        columns = pl.ds(pl.multiple_of(start + q * LANES, LANES), 2 * here)
        term = jnp.dot(
            weights_ref[:, q * DEPTH : (q + 1) * DEPTH],
            hankel_ref[0, :, columns],
            preferred_element_type=jnp.float32,
        )
        total = term if total is None else total + term
    out_ref[0, 0] = total[:, :here].astype(jnp.bfloat16)
    out_ref[1, 0] = total[:, here:].astype(jnp.bfloat16)


def long_series(weights, matrix, count, here):
    rows, taps = weights.shape
    detectors, depth, width = matrix.shape
    return pl.pallas_call(
        long_series_kernel,
        grid=(detectors, count // 2),
        in_specs=[
            pl.BlockSpec((rows, taps), lambda d, n: (0, 0)),
            pl.BlockSpec((1, depth, width), lambda d, n: (d, 0, 0)),
        ],
        out_specs=pl.BlockSpec((2, 1, rows, here), lambda d, n: (n, d, 0, 0)),
        out_shape=jax.ShapeDtypeStruct((count, detectors, rows, here), jnp.bfloat16),
        cost_estimate=COST,
        compiler_params=pltpu.CompilerParams(vmem_limit_bytes=32 * MIB),
        name="long_series",
    )(weights, matrix)


def shards(strain, basis_filters, coefficients):
    detectors, samples_here = strain.shape
    here = samples_here // STRIDE
    filters, taps = basis_filters.shape
    own_rows = coefficients.shape[0]
    count = lax.axis_size("tm")
    me = lax.axis_index("tm")
    group = lax.axis_index("basis")
    short = count == 8 and here == LANES

    def theirs(start, rows, *earlier):
        source = after(coefficients, *earlier) if earlier else coefficients
        at = (group // 2 ^ 1) * (2 * filters)
        return lax.dynamic_slice(source, (start, at), (rows, 2 * filters))

    sibling = flipped(basis_filters, "basis", 1)
    if not (short and own_rows == 256):
        chip_filters, own = staged(coefficients, basis_filters, sibling)
        answer = partial_rows(flipped(theirs(0, own_rows), "basis", 2), chip_filters)
        other = flipped(answer, "basis", 2).astype(jnp.float32)
        matrix = long_hankel(strain, taps, count * here)
        blocks = long_series((own + other).astype(jnp.bfloat16), matrix, count, here)
        arrived = lax.all_to_all(blocks, "tm", split_axis=0, concat_axis=0, tiled=True)
        return arrived.transpose(0, 2, 1, 3).reshape(count * own_rows, detectors, here)

    starts = [sum(SIZES[:g]) for g in range(len(SIZES))]
    cuts = [theirs(0, SIZES[0])]
    two = doubled(after(strain, cuts[0])[None])
    cuts.append(theirs(starts[1], SIZES[1], two))
    chip_filters, own = staged(after(coefficients, cuts[1]), basis_filters, sibling)
    cuts.append(theirs(starts[2], SIZES[2], own))
    waiting = [flipped(cut, "basis", 2) for cut in cuts]

    def answered(c, *earlier):
        answer = partial_rows(after(waiting[c], *earlier), chip_filters)
        return answer, flipped(answer, "basis", 2)

    four = doubled(after(two, own))
    answer_0, other_0 = answered(0, waiting[1], four)
    eight = doubled(after(four, answer_0))
    waiting.append(flipped(theirs(starts[3], SIZES[3], answer_0), "basis", 2))
    answer_1, other_1 = answered(1, waiting[2], answer_0)
    matrix = hankel(after(eight, answer_1), taps)
    answer_2, other_2 = answered(2, matrix)

    def along_z(pair, k):
        return flipped(pair, "tm", 2 * k)

    operands, places = [], []

    def place(operand, sources, start):
        places.extend((len(operands), i, k, start) for i, k in enumerate(sources))
        operands.append(operand)

    far_a = series(own, starts[0], [other_0], matrix, here, [(6, 7), (4, 5)])
    sent_a = [along_z(far_a[0], 3), along_z(far_a[1], 2)]
    _, other_3 = answered(3, answer_2, *sent_a)
    far_b = series(own, starts[1], [other_1], matrix, here, [(6, 7), (4, 5)])
    sent_b = [along_z(far_b[0], 3), along_z(far_b[1], 2)]
    rest = [after(other_2, sent_b[0], *sent_a), other_3]
    far_c = series(own, starts[2], rest, matrix, here, [(6,), (7,), (4,), (5,)])
    sent_c = [flipped(block, "tm", k) for block, k in zip(far_c, (6, 7, 4, 5))]
    rest = [after(other_0, far_c[0]), other_1, other_2, other_3]
    near = series(own, starts[0], rest, matrix, here, [(2,), (3,), (1,), (0,)])
    near = list(near)
    near[1], near[2] = after(near[1], sent_c[1]), after(near[2], sent_c[1])
    near = [flipped(block, "tm", k) if k else block for block, k in zip(near, (2, 3, 1, 0))]
    held = after(sent_a[0], near[3])
    halves = second_halves([[sent_a[1], sent_b[1]], [held, sent_b[0]]])
    for i, k in enumerate((6, 4)):
        place(sent_a[i], [k], starts[0])
        place(sent_b[i], [k], starts[1])
    for block, k in zip(sent_c, (6, 7, 4, 5)):
        place(block, [k], starts[2])
    place(flipped(halves, "tm", 1), [5, 7], starts[0])
    for block, k in zip(near, (2, 3, 1, 0)):
        place(block, [k], starts[0])
    return assembled(operands, places, count, own_rows).transpose(1, 0, 2)


def solution(mesh):
    placed = (P(None, "tm"), P("basis", None), P(("basis", "tm"), None))
    return jax.shard_map(
        shards, mesh=mesh, in_specs=placed, out_specs=P("basis", None, "tm"), check_vma=False
    )
```

```python
import functools

import jax
import jax.numpy as jnp
from jax import lax
from jax.experimental import pallas as pl
from jax.experimental.pallas import tpu as pltpu
from jax.sharding import PartitionSpec as P

STRIDE = 4
LANES = 128
DEPTH = 4 * LANES
MIB = 1024 * 1024
COST = pl.CostEstimate(flops=1, bytes_accessed=1, transcendentals=0)
SIZES = [64, 64, 64, 64]


def flipped(block, axis, mask):
    return lax.ppermute(block, axis, [(i, i ^ mask) for i in range(lax.axis_size(axis))])


def after(value, *others):
    return lax.optimization_barrier((value, *others))[0]


def in_vmem(array):
    return pltpu.with_memory_space_constraint(array, pltpu.VMEM)


def in_hbm(array):
    return pltpu.with_memory_space_constraint(array, pltpu.HBM)


def whole_in_vmem(count):
    return [pl.BlockSpec(memory_space=pltpu.VMEM)] * count


def doubled(blocks):
    return jnp.concatenate([blocks, flipped(blocks, "tm", blocks.shape[0])], axis=0)


def shifted(tile, distance):
    return pltpu.roll(tile, tile.shape[1] - distance, 1) if distance else tile


def hankel_kernel(strain_ref, out_ref, split_ref, tile_ref):
    count, _, samples = strain_ref.shape
    here = samples // STRIDE
    detectors, _, width = out_ref.shape
    me = lax.axis_index("tm")
    sample = lax.broadcasted_iota(jnp.int32, (samples, samples), 0)
    column = lax.broadcasted_iota(jnp.int32, (samples, samples), 1)
    wanted = STRIDE * lax.rem(column, here) + column // here
    selector = jnp.where(sample == wanted, 1.0, 0.0).astype(jnp.bfloat16)
    for k in range(count):
        split_ref[k] = jnp.dot(strain_ref[k], selector, preferred_element_type=jnp.float32)
    tile_ref[...] = jnp.zeros_like(tile_ref)
    for t in range(count):
        block = split_ref[me ^ t]
        for d in range(detectors):
            for p in range(STRIDE):
                tile_ref[d, p : p + 1, t * here : (t + 1) * here] = block[
                    d : d + 1, p * here : (p + 1) * here
                ]
    per_half = 8 // STRIDE
    row = lax.broadcasted_iota(jnp.int32, tile_ref.shape[1:], 0)
    for d in range(detectors):
        tile = tile_ref[d]
        tile = jnp.where(row < STRIDE, tile, pltpu.roll(shifted(tile, 1), STRIDE, 0))
        for i in range(out_ref.shape[1] // 16):
            first = shifted(tile, 2 * per_half * i)
            second = shifted(tile, 2 * per_half * i + per_half)
            block = jnp.concatenate([first[:, :width], second[:, :width]], axis=0)
            out_ref[d, 16 * i : 16 * (i + 1), :] = block.astype(out_ref.dtype)


def hankel(blocks, taps):
    count, detectors, samples = blocks.shape
    filled = jnp.pad(blocks, ((0, 0), (0, 16 - detectors), (0, 0)))
    width = count * samples // STRIDE + (taps - DEPTH) // STRIDE
    length = -(-(width + DEPTH // STRIDE) // LANES) * LANES
    return pl.pallas_call(
        hankel_kernel,
        in_specs=whole_in_vmem(1),
        out_specs=pl.BlockSpec(memory_space=pltpu.VMEM),
        out_shape=jax.ShapeDtypeStruct((detectors, DEPTH, width), jnp.bfloat16),
        scratch_shapes=[
            pltpu.VMEM(filled.shape, jnp.float32),
            pltpu.VMEM((detectors, 2 * STRIDE, length), jnp.float32),
        ],
        cost_estimate=COST,
        compiler_params=pltpu.CompilerParams(vmem_limit_bytes=16 * MIB),
        name="hankel",
    )(in_vmem(filled))


def long_hankel_kernel(rows_ref, out_ref):
    tile = rows_ref[0]
    width = out_ref.shape[2]
    length = tile.shape[1]
    per_half = 8 // STRIDE

    def step(i, carry):
        first = pltpu.roll(tile, lax.rem(length - 2 * per_half * i, length), 1)
        second = pltpu.roll(tile, length - 2 * per_half * i - per_half, 1)
        block = jnp.concatenate([first[:, :width], second[:, :width]], axis=0)
        out_ref[0, pl.ds(pl.multiple_of(16 * i, 16), 16), :] = block.astype(out_ref.dtype)
        return carry

    lax.fori_loop(0, out_ref.shape[1] // 16, step, 0)


def long_hankel(strain, taps, times):
    detectors, here = strain.shape
    phases = strain.reshape(detectors, here // STRIDE, STRIDE).transpose(0, 2, 1)
    phases = lax.all_gather(phases, "tm", axis=2, tiled=True)
    width = times + (taps - DEPTH) // STRIDE
    length = -(-(width + DEPTH // STRIDE) // LANES) * LANES
    padded = jnp.pad(phases.astype(jnp.float32), ((0, 0), (0, 0), (0, length + 1 - times)))
    rows = jnp.concatenate([padded[:, :, :length], padded[:, :, 1:]], axis=1)
    return pl.pallas_call(
        long_hankel_kernel,
        grid=(detectors,),
        in_specs=[pl.BlockSpec((1, 2 * STRIDE, length), lambda d: (d, 0, 0))],
        out_specs=pl.BlockSpec((1, DEPTH, width), lambda d: (d, 0, 0)),
        out_shape=jax.ShapeDtypeStruct((detectors, DEPTH, width), jnp.bfloat16),
        cost_estimate=COST,
        compiler_params=pltpu.CompilerParams(vmem_limit_bytes=24 * MIB),
        name="long_hankel",
    )(rows)


def staging_kernel(coefficients_ref, near_ref, far_ref, filters_ref, own_ref, rows_ref, semaphores):
    half, taps = near_ref.shape
    block = taps // 4
    group = lax.axis_index("basis")
    copies = []
    for i, which in enumerate((group, group ^ 1)):
        columns = pl.ds(pl.multiple_of(which * half, LANES), half)
        copies.append(
            pltpu.make_async_copy(
                coefficients_ref.at[:, columns],
                rows_ref.at[:, i * half : (i + 1) * half],
                semaphores.at[i],
            )
        )
    for n in range(4):
        for i, source in enumerate((near_ref, far_ref)):
            there = filters_ref.at[i * half : (i + 1) * half, n * block : (n + 1) * block]
            copies.append(
                pltpu.make_async_copy(
                    source.at[:, n * block : (n + 1) * block], there, semaphores.at[2 + 2 * n + i]
                )
            )
    for copy in copies:
        copy.start()
    copies[0].wait()
    copies[1].wait()
    for n in range(4):
        copies[2 + 2 * n].wait()
        copies[3 + 2 * n].wait()
        own_ref[:, n * block : (n + 1) * block] = jnp.dot(
            rows_ref[...],
            filters_ref[:, n * block : (n + 1) * block],
            preferred_element_type=jnp.float32,
        )


def staged(coefficients, near, far):
    own_rows = coefficients.shape[0]
    half, taps = near.shape
    return pl.pallas_call(
        staging_kernel,
        in_specs=[pl.BlockSpec(memory_space=pl.ANY)] * 3,
        out_specs=whole_in_vmem(2),
        out_shape=[
            jax.ShapeDtypeStruct((2 * half, taps), jnp.bfloat16),
            jax.ShapeDtypeStruct((own_rows, taps), jnp.float32),
        ],
        scratch_shapes=[
            pltpu.VMEM((own_rows, 2 * half), jnp.bfloat16),
            pltpu.SemaphoreType.DMA((10,)),
        ],
        cost_estimate=COST,
        compiler_params=pltpu.CompilerParams(vmem_limit_bytes=20 * MIB),
        name="staged",
    )(in_hbm(coefficients), in_hbm(near), in_hbm(far))


def partial_kernel(rows_ref, filters_ref, out_ref):
    depth, taps = filters_ref.shape
    core = lax.rem(lax.axis_index("basis"), 2)
    near = pl.ds(pl.multiple_of(core * (depth // 2), LANES), depth // 2)
    far = pl.ds(pl.multiple_of((1 - core) * (depth // 2), LANES), depth // 2)
    rows = jnp.concatenate([rows_ref[:, near], rows_ref[:, far]], axis=1)
    for n in range(0, taps, 512):
        out_ref[:, n : n + 512] = jnp.dot(
            rows, filters_ref[:, n : n + 512], preferred_element_type=jnp.float32
        ).astype(out_ref.dtype)


def partial_rows(rows, filters):
    count = rows.shape[0]
    depth, taps = filters.shape
    return pl.pallas_call(
        partial_kernel,
        in_specs=whole_in_vmem(2),
        out_specs=pl.BlockSpec(memory_space=pltpu.VMEM),
        out_shape=jax.ShapeDtypeStruct((count, taps), jnp.bfloat16),
        cost_estimate=COST,
        compiler_params=pltpu.CompilerParams(vmem_limit_bytes=16 * MIB),
        name="partial_rows",
    )(in_vmem(rows), in_vmem(filters))


def series_kernel(start, parts, far, targets, own_ref, *refs):
    others, hankel_ref, outs, scratch = refs[:parts], refs[parts], refs[parts + 1 : -1], refs[-1]
    detectors = hankel_ref.shape[0]
    rows, times = scratch.shape
    taps = own_ref.shape[1]
    here = outs[0].shape[-1]
    near = times // here
    me = lax.axis_index("tm")
    half = me // near
    first = (1 - half if far else half) * times
    other = jnp.concatenate([ref[...] for ref in others], axis=0)
    weights = (own_ref[start : start + rows] + other.astype(jnp.float32)).astype(jnp.bfloat16)
    for d in range(detectors):
        total = None
        for q in range(taps // DEPTH):
            columns = pl.ds(pl.multiple_of(first + q * LANES, LANES), times)
            term = jnp.dot(
                weights[:, q * DEPTH : (q + 1) * DEPTH],
                hankel_ref[d, :, columns],
                preferred_element_type=jnp.float32,
            )
            total = term if total is None else total + term
        scratch[...] = total.astype(jnp.bfloat16)
        for out, target in zip(outs, targets):
            for s, k in enumerate(target):
                at = pl.multiple_of(lax.rem(me ^ k, near) * here, LANES)
                out[s, d] = scratch[:, pl.ds(at, here)]


def series(own, start, others, matrix, here, targets):
    taps = own.shape[1]
    rows = sum(part.shape[0] for part in others)
    detectors = matrix.shape[0]
    near = 4
    far = targets[0][0] >= near
    shapes = [(len(target), detectors, rows, here) for target in targets]
    return pl.pallas_call(
        functools.partial(series_kernel, start, len(others), far, targets),
        in_specs=whole_in_vmem(2 + len(others)),
        out_specs=whole_in_vmem(len(targets)),
        out_shape=[jax.ShapeDtypeStruct(shape, jnp.bfloat16) for shape in shapes],
        scratch_shapes=[pltpu.VMEM((rows, near * here), jnp.bfloat16)],
        cost_estimate=COST,
        compiler_params=pltpu.CompilerParams(vmem_limit_bytes=16 * MIB),
        name="series",
    )(in_vmem(own), *[in_vmem(part) for part in others], in_vmem(matrix))


def second_halves_kernel(counts, *refs):
    ins, out_ref = list(refs[:-1]), refs[-1]
    for k, count in enumerate(counts):
        start = 0
        for ref in ins[:count]:
            rows = ref.shape[2]
            out_ref[k, :, start : start + rows] = ref[1]
            start += rows
        ins = ins[count:]


def second_halves(columns):
    detectors, _, here = columns[0][0].shape[1:]
    rows = sum(pair.shape[2] for pair in columns[0])
    pairs = [pair for column in columns for pair in column]
    return pl.pallas_call(
        functools.partial(second_halves_kernel, [len(column) for column in columns]),
        in_specs=whole_in_vmem(len(pairs)),
        out_specs=pl.BlockSpec(memory_space=pltpu.VMEM),
        out_shape=jax.ShapeDtypeStruct((len(columns), detectors, rows, here), jnp.bfloat16),
        cost_estimate=COST,
        compiler_params=pltpu.CompilerParams(vmem_limit_bytes=16 * MIB),
        name="second_halves",
    )(*[in_vmem(pair) for pair in pairs])


def assembling_kernel(places, own_rows, *refs):
    blocks, out_ref, semaphores = refs[:-2], refs[-2], refs[-1]
    me = lax.axis_index("tm")
    copies = []
    for i, (operand, index, k, start) in enumerate(places):
        block = blocks[operand].at[index]
        rows = block.shape[1]
        at = pl.multiple_of((me ^ k) * own_rows + start, 16)
        copies.append(
            pltpu.make_async_copy(
                block, out_ref.at[:, pl.ds(at, rows), :], semaphores.at[i]
            )
        )
    for copy in copies:
        copy.start()
    for copy in copies:
        copy.wait()


def assembled(operands, places, count, own_rows):
    detectors, _, here = operands[0].shape[-3:]
    return pl.pallas_call(
        functools.partial(assembling_kernel, places, own_rows),
        in_specs=whole_in_vmem(len(operands)),
        out_specs=pl.BlockSpec(memory_space=pl.ANY),
        out_shape=jax.ShapeDtypeStruct((detectors, count * own_rows, here), jnp.bfloat16),
        scratch_shapes=[pltpu.SemaphoreType.DMA((len(places),))],
        cost_estimate=COST,
        compiler_params=pltpu.CompilerParams(vmem_limit_bytes=16 * MIB),
        name="assembled",
    )(*[in_vmem(operand) for operand in operands])


def long_series_kernel(weights_ref, hankel_ref, out_ref):
    here = out_ref.shape[3]
    start = pl.program_id(1) * (2 * here)
    total = None
    for q in range(weights_ref.shape[1] // DEPTH):
        columns = pl.ds(pl.multiple_of(start + q * LANES, LANES), 2 * here)
        term = jnp.dot(
            weights_ref[:, q * DEPTH : (q + 1) * DEPTH],
            hankel_ref[0, :, columns],
            preferred_element_type=jnp.float32,
        )
        total = term if total is None else total + term
    out_ref[0, 0] = total[:, :here].astype(jnp.bfloat16)
    out_ref[1, 0] = total[:, here:].astype(jnp.bfloat16)


def long_series(weights, matrix, count, here):
    rows, taps = weights.shape
    detectors, depth, width = matrix.shape
    return pl.pallas_call(
        long_series_kernel,
        grid=(detectors, count // 2),
        in_specs=[
            pl.BlockSpec((rows, taps), lambda d, n: (0, 0)),
            pl.BlockSpec((1, depth, width), lambda d, n: (d, 0, 0)),
        ],
        out_specs=pl.BlockSpec((2, 1, rows, here), lambda d, n: (n, d, 0, 0)),
        out_shape=jax.ShapeDtypeStruct((count, detectors, rows, here), jnp.bfloat16),
        cost_estimate=COST,
        compiler_params=pltpu.CompilerParams(vmem_limit_bytes=32 * MIB),
        name="long_series",
    )(weights, matrix)


def shards(strain, basis_filters, coefficients):
    detectors, samples_here = strain.shape
    here = samples_here // STRIDE
    filters, taps = basis_filters.shape
    own_rows = coefficients.shape[0]
    count = lax.axis_size("tm")
    me = lax.axis_index("tm")
    group = lax.axis_index("basis")
    short = count == 8 and here == LANES

    def theirs(start, rows, *earlier):
        source = after(coefficients, *earlier) if earlier else coefficients
        at = (group // 2 ^ 1) * (2 * filters)
        return lax.dynamic_slice(source, (start, at), (rows, 2 * filters))

    sibling = flipped(basis_filters, "basis", 1)
    if not (short and own_rows == 256):
        chip_filters, own = staged(coefficients, basis_filters, sibling)
        answer = partial_rows(flipped(theirs(0, own_rows), "basis", 2), chip_filters)
        other = flipped(answer, "basis", 2).astype(jnp.float32)
        matrix = long_hankel(strain, taps, count * here)
        blocks = long_series((own + other).astype(jnp.bfloat16), matrix, count, here)
        arrived = lax.all_to_all(blocks, "tm", split_axis=0, concat_axis=0, tiled=True)
        return arrived.transpose(0, 2, 1, 3).reshape(count * own_rows, detectors, here)

    starts = [sum(SIZES[:g]) for g in range(len(SIZES))]
    cuts = [theirs(0, SIZES[0])]
    two = doubled(after(strain, cuts[0])[None])
    cuts.append(theirs(starts[1], SIZES[1], two))
    chip_filters, own = staged(after(coefficients, cuts[1]), basis_filters, sibling)
    cuts.append(theirs(starts[2], SIZES[2], own))
    waiting = [flipped(cut, "basis", 2) for cut in cuts]

    def answered(c, *earlier):
        answer = partial_rows(after(waiting[c], *earlier), chip_filters)
        return answer, flipped(answer, "basis", 2)

    four = doubled(after(two, own))
    answer_0, other_0 = answered(0, waiting[1], four)
    eight = doubled(after(four, answer_0))
    waiting.append(flipped(theirs(starts[3], SIZES[3], answer_0), "basis", 2))
    answer_1, other_1 = answered(1, waiting[2], answer_0)
    matrix = hankel(after(eight, answer_1), taps)
    answer_2, other_2 = answered(2, matrix)

    def along_z(pair, k):
        return flipped(pair, "tm", 2 * k)

    operands, places = [], []

    def place(operand, sources, start):
        places.extend((len(operands), i, k, start) for i, k in enumerate(sources))
        operands.append(operand)

    far_a = series(own, starts[0], [other_0], matrix, here, [(6, 7), (4, 5)])
    sent_a = [along_z(far_a[0], 3), along_z(far_a[1], 2)]
    _, other_3 = answered(3, answer_2, *sent_a)
    far_b = series(own, starts[1], [other_1], matrix, here, [(6, 7), (4, 5)])
    sent_b = [along_z(far_b[0], 3), along_z(far_b[1], 2)]
    rest = [after(other_2, sent_b[0], *sent_a), other_3]
    far_c = series(own, starts[2], rest, matrix, here, [(6,), (7,), (4,), (5,)])
    sent_c = [flipped(block, "tm", k) for block, k in zip(far_c, (6, 7, 4, 5))]
    rest = [after(other_0, far_c[0]), other_1, other_2, other_3]
    near = series(own, starts[0], rest, matrix, here, [(2,), (3,), (1,), (0,)])
    near = list(near)
    near[1], near[2] = after(near[1], sent_c[1]), after(near[2], sent_c[1])
    near = [flipped(block, "tm", k) if k else block for block, k in zip(near, (2, 3, 1, 0))]
    held = after(sent_a[0], near[3])
    halves = second_halves([[sent_a[1], sent_b[1]], [held, sent_b[0]]])
    for i, k in enumerate((6, 4)):
        place(sent_a[i], [k], starts[0])
        place(sent_b[i], [k], starts[1])
    for block, k in zip(sent_c, (6, 7, 4, 5)):
        place(block, [k], starts[2])
    place(flipped(halves, "tm", 1), [5, 7], starts[0])
    for block, k in zip(near, (2, 3, 1, 0)):
        place(block, [k], starts[0])
    return assembled(operands, places, count, own_rows).transpose(1, 0, 2)


def solution(mesh):
    placed = (P(None, "tm"), P("basis", None), P(("basis", "tm"), None))
    return jax.shard_map(
        shards, mesh=mesh, in_specs=placed, out_specs=P("basis", None, "tm"), check_vma=False
    )
```
